128 devices in a mesh: row: 8 (over y, z_hi), col: 16 (over z_lo, x, core).
Axes of the slice: x: 4, y: 4, z: 4 (z_hi: 2, z_lo: 2; z = z_hi * 2 + z_lo), core: 2. Of those that a mesh axis runs over, the one named last changes fastest.
Arguments:
- orbitals: float32 [256, 256, 2048], P(None, ('row', 'col')), may hold values from -53 to 53, as said below
- potential: float32 [256, 2048], P(('row', 'col')), may hold values from 0.5 to 4
Outputs:
- correlation: float32 [256, 256], P(('row', 'col'))
- projected: float32 [256, 256], P(('row', 'col'))
- relayed: float32 [256, 256, 2048], P('col', 'row')
- relayed_applied: float32 [256, 256, 2048], P('col', 'row')
The draws below stay inside these ranges and needn't reach their ends.
Inputs may be any that keep to these rules, and one draw needn't show every extreme that they name: `orbitals`: real values.
All inputs are finite; a program needn't handle non-finite values.
Results may differ from the reference program's by a relative error of at most 0.00007.
Values sent between devices are 32-bit elements; how exact they have to be, the bound alone decides.
No kernel may reach another device: no remote copies, remote signals or barrier semaphores. Data moves between devices by JAX's collectives and lax.ppermute only.
A program may use at most 128 MiB of HBM per device.

```python
import math
import jax
import jax.numpy as jnp
from jax import lax

M = 256
P_SIZE = 2048
NX = 256


def draw_orbitals(key, part):
    key = jax.random.fold_in(key, 11)
    key_a, key_b, key_c, key_d = jax.random.split(key, 4)
    random_part = jnp.clip(jax.random.normal(key_a, (M, NX, P_SIZE), jnp.float32), -6.0, 6.0)
    shared = jnp.clip(jax.random.normal(key_b, (NX, P_SIZE), jnp.float32), -6.0, 6.0)
    envelope = jnp.exp(jax.random.uniform(key_d, (NX,), jnp.float32, math.log(0.3), math.log(3.0)))
    amplitude = jnp.clip(0.5 * jax.random.normal(key_c, (M,), jnp.float32), -1.5, 1.5)
    blended = random_part + 0.4 * jnp.roll(random_part, 1, axis=0) + amplitude[:, None, None] * shared[None]
    return (envelope[None, :, None] * blended).astype(jnp.float32)


def steps_of(rng, shape, pieces, low, top_value):
    def one(dim, blocks):
        draws = jax.random.uniform(jax.random.fold_in(jax.random.fold_in(rng, 6), dim), (blocks,), jnp.float32, low / len(pieces), top_value / len(pieces))
        return jnp.repeat(jnp.exp(draws), shape[dim] // blocks).reshape((-1,) + (1,) * (len(shape) - dim - 1))

    gain = one(*pieces[0])
    for cut in pieces[1:]:
        gain = gain * one(*cut)
    return gain


def setup_inputs(seed: int = 0) -> dict:
    keys = jax.random.split(jax.random.key(seed), 3)
    orbitals = draw_orbitals(jax.random.fold_in(keys[2], 71), 0)
    potential = jnp.clip(jnp.exp(math.log(4.0) - 2.0794415 * jax.random.uniform(keys[1], (NX, P_SIZE), jnp.float32) ** steps_of(keys[1], (NX, P_SIZE), ((0, 128),), -0.2, 0.2)), 0.5, 4.0)
    return dict(orbitals=orbitals, potential=potential)


def apply_hamiltonian(orbitals, potential):
    padded = jnp.pad(orbitals, ((0, 0), (1, 1), (0, 0)))
    across = padded[:, 2:, :] + padded[:, :-2, :]
    within = jnp.roll(orbitals, 1, axis=2) + jnp.roll(orbitals, -1, axis=2)
    return (2.0 + potential)[None] * orbitals - 0.5 * across - 0.5 * within


def reference(orbitals, potential):
    applied = apply_hamiltonian(orbitals, potential)
    points = NX * P_SIZE
    flattened = orbitals.reshape(M, points)
    applied_flat = applied.reshape(M, points)
    correlation = lax.dot_general(flattened, flattened, (((1,), (1,)), ((), ())), precision=lax.Precision.HIGHEST, preferred_element_type=jnp.float32) / points
    projected = lax.dot_general(flattened, applied_flat, (((1,), (1,)), ((), ())), precision=lax.Precision.HIGHEST, preferred_element_type=jnp.float32) / points
    return correlation, projected, orbitals, applied
```

```python
import functools

import jax
import jax.numpy as jnp
from jax import lax
from jax.experimental import pallas as pl
from jax.experimental.pallas import tpu as pltpu
from jax.sharding import PartitionSpec as P

LANES = 128
NT = (((1,), (1,)), ((), ()))


def tile_view(x):
    *lead, planes, points = x.shape
    tiles = points // LANES
    n = len(lead)
    x = x.reshape(*lead, planes, tiles, LANES)
    x = x.transpose(*range(n), n + 1, n, n + 2)
    return x.reshape(*lead, tiles * planes, LANES)


def split(x):
    high = x.astype(jnp.bfloat16)
    return high, (x - high.astype(jnp.float32)).astype(jnp.bfloat16)


def extract_kernel(count, rows, x_ref, first_ref, last_ref):
    half = rows // 4
    for o in range(count):
        first_ref[pl.ds(o * half, half), :] = x_ref[pl.ds(o * rows, half, stride=2), :]
        last_ref[pl.ds(o * half, half), :] = x_ref[pl.ds(o * rows + 2 * half + 1, half, stride=2), :]


def extract(x, count, rows):
    block = 32
    half = rows // 4
    return pl.pallas_call(
        functools.partial(extract_kernel, block, rows),
        grid=(count // block,),
        in_specs=[pl.BlockSpec((block * rows, LANES), lambda i: (i, 0))],
        out_specs=[pl.BlockSpec((block * half, LANES), lambda i: (i, 0))] * 2,
        out_shape=[jax.ShapeDtypeStruct((count * half, LANES), jnp.float32)] * 2,
        cost_estimate=pl.CostEstimate(flops=0, bytes_accessed=count * rows * LANES * 8, transcendentals=0),
    )(x)


def gram_kernel(count, rows, scale, x_ref, v_ref, after_ref, before_ref, g_ref):
    tiles = rows // 2
    half = tiles // 2
    lane = lax.broadcasted_iota(jnp.int32, (count, LANES), 1)

    def load(t, p):
        return x_ref[pl.ds(2 * t + p, count, stride=rows), :]

    def rolled(t, p):
        return pltpu.roll(load(t % tiles, p), LANES - 1, 1)

    step = 4
    with_self = with_low = with_half = None
    now = [rolled(0, p) for p in (0, 1)]
    for begin in range(0, tiles, step):
        xs, bs = [], []
        for t in range(begin, begin + step):
            here = [load(t, p) for p in (0, 1)]
            later = [rolled(t + 1, p) for p in (0, 1)]
            for p in (0, 1):
                beside = jnp.where(lane == LANES - 1, later[p], now[p])
                if p == 0:
                    beside = beside + here[1]
                if p == 1 and t < half:
                    beside = beside + after_ref[pl.ds(t, count, stride=half), :]
                if p == 0 and t >= half:
                    beside = beside + before_ref[pl.ds(t - half, count, stride=half), :]
                factor = 1.0 + 0.5 * v_ref[pl.ds(2 * t + p, 1), :]
                xs.append(here[p])
                bs.append(factor * here[p] - 0.5 * beside)
            now = later
        x_high, x_low = split(jnp.concatenate(xs, axis=1))
        b_high, b_low = split(jnp.concatenate(bs, axis=1))
        dot = functools.partial(lax.dot_general, dimension_numbers=NT, preferred_element_type=jnp.float32)
        a = dot(x_high, x_high)
        l = dot(x_high, x_low)
        q = dot(x_high, b_high) + dot(x_high, b_low) + dot(x_low, b_high)
        with_self = a if with_self is None else with_self + a
        with_low = l if with_low is None else with_low + l
        with_half = q if with_half is None else with_half + q
    g_ref[:, :count] = (with_self + with_low + with_low.T) * scale
    g_ref[:, count:] = (with_half + with_half.T) * scale


def gram(x, v, after, before, count, rows, scale):
    return pl.pallas_call(
        functools.partial(gram_kernel, count, rows, scale),
        out_shape=jax.ShapeDtypeStruct((count, 2 * count), jnp.float32),
        in_specs=[pl.BlockSpec(memory_space=pltpu.VMEM)] * 4,
        out_specs=pl.BlockSpec(memory_space=pltpu.VMEM),
        compiler_params=pltpu.CompilerParams(vmem_limit_bytes=48 * 2**20),
        cost_estimate=pl.CostEstimate(
            flops=10 * count * count * rows * LANES, bytes_accessed=count * rows * LANES * 6, transcendentals=0
        ),
    )(x, v, after, before)


def interleaved(source_ref, start, stride, sources, tiles, work_ref):
    planes = 2 * sources
    for t in range(tiles):
        for p in (0, 1):
            for h in range(0, sources, 8):
                work_ref[pl.ds(planes * t + 2 * h + p, 8, stride=2), :] = source_ref[
                    pl.ds(start + h * stride + 2 * t + p, 8, stride=stride), :
                ]
    return jnp.concatenate([work_ref[pl.ds(planes * t, planes), :] for t in range(tiles)], axis=1)


def block_kernel(sources, block, rows, x_ref, v_ref, before_ref, after_ref, out_ref, applied_ref, v_scr, work_ref):
    tiles = rows // 2
    planes = 2 * sources

    @pl.when(pl.program_id(0) == 0)
    def _():
        v_scr[...] = 2.0 + interleaved(v_ref, 0, rows, sources, tiles, work_ref.at[0])

    flat = x_ref.reshape(sources * block * rows, LANES)
    row = lax.broadcasted_iota(jnp.int32, (planes, tiles * LANES), 0)
    for o in range(block):
        psi = interleaved(flat, o * rows, block * rows, sources, tiles, work_ref.at[o])
        out_ref[o] = psi
        down = jnp.where(row == 0, before_ref[pl.ds(o, 1), :], pltpu.roll(psi, 1, 0))
        up = jnp.where(row == planes - 1, after_ref[pl.ds(o, 1), :], pltpu.roll(psi, planes - 1, 0))
        beside = pltpu.roll(psi, 1, 1) + pltpu.roll(psi, tiles * LANES - 1, 1)
        applied_ref[o] = v_scr[...] * psi - 0.5 * (down + up) - 0.5 * beside


def to_block(x, v, before, after):
    sources, count, rows, _ = x.shape
    block = 2
    points = rows // 2 * LANES
    out = jax.ShapeDtypeStruct((count, 2 * sources, points), jnp.float32)
    before = before.reshape(count // block, block, points)
    after = after.reshape(count // block, block, points)
    edge = pl.BlockSpec((None, block, points), lambda i: (i, 0, 0))
    return pl.pallas_call(
        functools.partial(block_kernel, sources, block, rows),
        grid=(count // block,),
        in_specs=[
            pl.BlockSpec((sources, block, rows, LANES), lambda i: (0, i, 0, 0)),
            pl.BlockSpec((sources * rows, LANES), lambda i: (0, 0)),
            edge,
            edge,
        ],
        out_specs=[pl.BlockSpec((block, 2 * sources, points), lambda i: (i, 0, 0))] * 2,
        out_shape=[out, out],
        scratch_shapes=[
            pltpu.VMEM((2 * sources, points), jnp.float32),
            pltpu.VMEM((block, sources * rows, LANES), jnp.float32),
        ],
        compiler_params=pltpu.CompilerParams(vmem_limit_bytes=32 * 2**20),
        cost_estimate=pl.CostEstimate(
            flops=10 * sources * count * rows * LANES,
            bytes_accessed=12 * sources * count * rows * LANES,
            transcendentals=0,
        ),
    )(x, v, before, after)


def local(orbitals, potential):
    count, planes, points = orbitals.shape
    every = ("row", "col")
    devices, n_row, n_col = lax.axis_size(every), lax.axis_size("row"), lax.axis_size("col")
    rows = planes * points // LANES
    scale = 1.0 / (devices * planes * points)
    forward = [(i, i + 1) for i in range(devices - 1)]
    backward = [(j, i) for i, j in forward]

    tiled = tile_view(orbitals).reshape(count * rows, LANES)
    first, last = extract(tiled, count, rows)
    after = lax.ppermute(first, every, backward)
    before = lax.ppermute(last, every, forward)
    received = lax.all_to_all(orbitals, "col", split_axis=0, concat_axis=0, tiled=True)
    received = received.reshape(n_col, count // n_col, planes, points)

    potentials = lax.all_gather(potential, "col", axis=0, tiled=False)

    g = gram(tiled, tile_view(potential), after, before, count, rows, scale)
    g = lax.all_to_all(g.reshape(n_row, count // n_row, 2 * count), "row", 0, 0).sum(axis=0)
    g = lax.all_to_all(g.reshape(n_col, count // devices, 2 * count), "col", 0, 0).sum(axis=0)

    up = [(i, i + 1) for i in range(n_row - 1)]
    down = [(j, i) for i, j in up]
    edge_before = lax.ppermute(received[n_col - 1, :, planes - 1, :], "row", up)
    edge_after = lax.ppermute(received[0, :, 0, :], "row", down)
    relayed, relayed_applied = to_block(
        tile_view(received), tile_view(potentials).reshape(n_col * rows, LANES), edge_before, edge_after
    )
    return g[:, :count], g[:, count:], relayed, relayed_applied


def solution(mesh):
    in_specs = (P(None, ("row", "col"), None), P(("row", "col"), None))
    out_specs = (
        P(("row", "col"), None),
        P(("row", "col"), None),
        P("col", "row", None),
        P("col", "row", None),
    )
    return jax.shard_map(local, mesh=mesh, in_specs=in_specs, out_specs=out_specs, check_vma=False)
```

```python
import functools

import jax
import jax.numpy as jnp
from jax import lax
from jax.experimental import pallas as pl
from jax.experimental.pallas import tpu as pltpu
from jax.sharding import PartitionSpec as P

LANES = 128
NT = (((1,), (1,)), ((), ()))


def tile_view(x):
    *lead, planes, points = x.shape
    tiles = points // LANES
    n = len(lead)
    x = x.reshape(*lead, planes, tiles, LANES)
    x = x.transpose(*range(n), n + 1, n, n + 2)
    return x.reshape(*lead, tiles * planes, LANES)


def split(x):
    high = x.astype(jnp.bfloat16)
    return high, (x - high.astype(jnp.float32)).astype(jnp.bfloat16)


def extract_kernel(count, rows, x_ref, v_ref, first_ref, last_ref, packed_ref):
    half = rows // 4
    for o in range(count):
        first_ref[pl.ds(o * half, half), :] = x_ref[pl.ds(o * rows, half, stride=2), :]
        last_ref[pl.ds(o * half, half), :] = x_ref[pl.ds(o * rows + 2 * half + 1, half, stride=2), :]
    parts, length = packed_ref.shape[0], count // packed_ref.shape[0] * rows
    for c in range(parts):
        packed_ref[c, :length] = x_ref[pl.ds(c * length, length), :]
        packed_ref[c, length:] = v_ref[...]


def extract(x, v, count, rows, parts):
    half = jax.ShapeDtypeStruct((count * rows // 4, LANES), jnp.float32)
    packed = jax.ShapeDtypeStruct((parts, (count // parts + 1) * rows, LANES), jnp.float32)
    return pl.pallas_call(
        functools.partial(extract_kernel, count, rows),
        in_specs=[pl.BlockSpec(memory_space=pltpu.VMEM)] * 2,
        out_specs=[pl.BlockSpec(memory_space=pltpu.VMEM)] * 3,
        out_shape=[half, half, packed],
        compiler_params=pltpu.CompilerParams(vmem_limit_bytes=16 * 2**20),
        cost_estimate=pl.CostEstimate(flops=0, bytes_accessed=count * rows * LANES * 10, transcendentals=0),
    )(x, v)


def gram_kernel(count, rows, scale, x_ref, v_ref, after_ref, before_ref, keep_ref, send_ref, work_ref):
    tiles = rows // 2
    half = tiles // 2
    lane = lax.broadcasted_iota(jnp.int32, (count, LANES), 1)

    def load(t, p):
        return x_ref[pl.ds(2 * t + p, count, stride=rows), :]

    def rolled(t, p):
        return pltpu.roll(load(t % tiles, p), LANES - 1, 1)

    step = 4
    with_self = with_low = with_half = None
    now = [rolled(0, p) for p in (0, 1)]
    for begin in range(0, tiles, step):
        xs, bs = [], []
        for t in range(begin, begin + step):
            here = [load(t, p) for p in (0, 1)]
            later = [rolled(t + 1, p) for p in (0, 1)]
            for p in (0, 1):
                beside = jnp.where(lane == LANES - 1, later[p], now[p])
                if p == 0:
                    beside = beside + here[1]
                if p == 1 and t < half:
                    beside = beside + after_ref[pl.ds(t, count, stride=half), :]
                if p == 0 and t >= half:
                    beside = beside + before_ref[pl.ds(t - half, count, stride=half), :]
                factor = 1.0 + 0.5 * v_ref[pl.ds(2 * t + p, 1), :]
                xs.append(here[p])
                bs.append(factor * here[p] - 0.5 * beside)
            now = later
        x_high, x_low = split(jnp.concatenate(xs, axis=1))
        b_high, b_low = split(jnp.concatenate(bs, axis=1))
        dot = functools.partial(lax.dot_general, dimension_numbers=NT, preferred_element_type=jnp.float32)
        a = dot(x_high, x_high)
        l = dot(x_high, x_low)
        q = dot(x_high, b_high) + dot(x_high, b_low) + dot(x_low, b_high)
        with_self = a if with_self is None else with_self + a
        with_low = l if with_low is None else with_low + l
        with_half = q if with_half is None else with_half + q
    first = (with_self + with_low + with_low.T) * scale
    second = (with_half + with_half.T) * scale
    blocks = count // LANES
    for m, matrix in enumerate((first, second)):
        for j in range(blocks):
            work_ref[m * blocks + j] = matrix[:, j * LANES : (j + 1) * LANES]
    core = lax.rem(lax.axis_index("col"), 2)
    chips = count // 4
    for ref, which in ((keep_ref, core), (send_ref, 1 - core)):
        for b in (0, 1):
            for j in range(2 * blocks):
                ref[:, pl.ds((b * 2 * blocks + j) * LANES, LANES)] = work_ref.at[j][
                    pl.ds(2 * which + b, chips, stride=4), :
                ]


def gram(x, v, after, before, count, rows, scale):
    part = jax.ShapeDtypeStruct((count // 4, 4 * count), jnp.float32)
    return pl.pallas_call(
        functools.partial(gram_kernel, count, rows, scale),
        out_shape=[part, part],
        in_specs=[pl.BlockSpec(memory_space=pltpu.VMEM)] * 4,
        out_specs=[pl.BlockSpec(memory_space=pltpu.VMEM)] * 2,
        scratch_shapes=[pltpu.VMEM((2 * count // LANES, count, LANES), jnp.float32)],
        compiler_params=pltpu.CompilerParams(vmem_limit_bytes=16 * 2**20),
        cost_estimate=pl.CostEstimate(
            flops=400 * count * count * rows * LANES, bytes_accessed=count * rows * LANES * 6, transcendentals=0
        ),
    )(x, v, after, before)


def edges_kernel(orbitals, rows, low_ref, high_ref, first_ref, last_ref):
    for t in range(rows // 2):
        lanes = pl.ds(t * LANES, LANES)
        first_ref[:, lanes] = low_ref[0, pl.ds(2 * t, orbitals, stride=rows), :]
        last_ref[:, lanes] = high_ref[0, pl.ds(2 * t + 1, orbitals, stride=rows), :]


def edges_of(received, orbitals, rows):
    sources, length, _ = received.shape
    out = jax.ShapeDtypeStruct((orbitals, rows // 2 * LANES), jnp.float32)
    return pl.pallas_call(
        functools.partial(edges_kernel, orbitals, rows),
        grid=(1,),
        in_specs=[
            pl.BlockSpec((1, length, LANES), lambda i: (0, 0, 0)),
            pl.BlockSpec((1, length, LANES), lambda i: (sources - 1, 0, 0)),
        ],
        out_specs=[pl.BlockSpec(out.shape, lambda i: (0, 0))] * 2,
        out_shape=[out, out],
        compiler_params=pltpu.CompilerParams(vmem_limit_bytes=8 * 2**20),
        cost_estimate=pl.CostEstimate(flops=0, bytes_accessed=2**18, transcendentals=0),
    )(received, received)


def block_kernel(sources, block, rows, x_ref, v_ref, out_ref, applied_ref, sides_ref, v_scr, work_ref):
    tiles, planes = rows // 2, 2 * sources
    points = tiles * LANES

    def interleaved(flat, start, stride, work):
        for k in range(sources):
            for q in range(0, tiles, 4):
                piece = flat[pl.ds(k * stride + start + 2 * q, 8), :]
                for i in range(4):
                    work[pl.ds(planes * (q + i) + 2 * k, 2), :] = piece[2 * i : 2 * i + 2, :]
        return jnp.concatenate([work[pl.ds(planes * t, planes), :] for t in range(tiles)], axis=1)

    @pl.when(pl.program_id(0) == 0)
    def _():
        v_scr[...] = 2.0 + interleaved(v_ref.reshape(sources * rows, LANES), 0, rows, work_ref.at[0])

    flat = x_ref.reshape(sources * block * rows, LANES)
    row = lax.broadcasted_iota(jnp.int32, (planes, points), 0)
    for o in range(block):
        psi = interleaved(flat, o * rows, block * rows, work_ref.at[o])
        out_ref[o] = psi
        down = jnp.where(row == 0, 0.0, pltpu.roll(psi, 1, 0))
        up = jnp.where(row == planes - 1, 0.0, pltpu.roll(psi, planes - 1, 0))
        beside = pltpu.roll(psi, 1, 1) + pltpu.roll(psi, points - 1, 1)
        applied = v_scr[...] * psi - 0.5 * (down + up) - 0.5 * beside
        applied_ref[o] = applied
        at = pl.program_id(0) * block + o
        sides_ref[0, at] = applied[:8]
        sides_ref[1, at] = applied[planes - 8 :]


def to_block(received, orbitals, rows):
    block, sources = 4, received.shape[0]
    planes, points = 2 * sources, rows // 2 * LANES
    received = received.reshape(sources, orbitals + 1, rows, LANES)
    out = jax.ShapeDtypeStruct((orbitals, planes, points), jnp.float32)
    return pl.pallas_call(
        functools.partial(block_kernel, sources, block, rows),
        grid=(orbitals // block,),
        in_specs=[
            pl.BlockSpec((sources, block, rows, LANES), lambda i: (0, i, 0, 0)),
            pl.BlockSpec((sources, 1, rows, LANES), lambda i: (0, orbitals, 0, 0)),
        ],
        out_specs=[pl.BlockSpec((block, planes, points), lambda i: (i, 0, 0))] * 2
        + [pl.BlockSpec(memory_space=pltpu.VMEM)],
        out_shape=[out, out, jax.ShapeDtypeStruct((2, orbitals, 8, points), jnp.float32)],
        scratch_shapes=[
            pltpu.VMEM((planes, points), jnp.float32),
            pltpu.VMEM((block, planes * points // LANES, LANES), jnp.float32),
        ],
        compiler_params=pltpu.CompilerParams(vmem_limit_bytes=24 * 2**20),
        cost_estimate=pl.CostEstimate(flops=0, bytes_accessed=12 * orbitals * planes * points, transcendentals=0),
    )(received, received)


def fix_kernel(before_ref, after_ref, sides_ref, applied_ref, out_ref, work_ref, sem):
    orbitals, planes, _ = applied_ref.shape
    copies = []
    for e, edge_ref in enumerate((before_ref, after_ref)):
        for o in range(orbitals):
            row = 7 * e
            work_ref[e, o] = sides_ref[e, o]
            work_ref[e, o, pl.ds(row, 1), :] = sides_ref[e, o, pl.ds(row, 1), :] - 0.5 * edge_ref[pl.ds(o, 1), :]
            target = out_ref.at[o, pl.ds(e * (planes - 8), 8), :]
            copies.append(pltpu.make_async_copy(work_ref.at[e, o], target, sem.at[e, o]))
            copies[-1].start()
    for copy in copies:
        copy.wait()


def fix_edges(applied, sides, before, after):
    orbitals, _, points = applied.shape
    return pl.pallas_call(
        fix_kernel,
        in_specs=[pl.BlockSpec(memory_space=pltpu.VMEM)] * 3 + [pl.BlockSpec(memory_space=pl.ANY)],
        out_specs=pl.BlockSpec(memory_space=pl.ANY),
        out_shape=jax.ShapeDtypeStruct(applied.shape, jnp.float32),
        input_output_aliases={3: 0},
        scratch_shapes=[
            pltpu.VMEM((2, orbitals, 8, points), jnp.float32),
            pltpu.SemaphoreType.DMA((2, orbitals)),
        ],
        compiler_params=pltpu.CompilerParams(vmem_limit_bytes=12 * 2**20),
        cost_estimate=pl.CostEstimate(flops=0, bytes_accessed=32 * orbitals * points, transcendentals=0),
    )(before, after, sides, applied)


def exchange(x, mask):
    every = ("row", "col")
    return lax.ppermute(x, every, [(i, i ^ mask) for i in range(lax.axis_size(every))])


def digit(position, radix):
    return (lax.axis_index(("row", "col")) // position) % radix


def reduce_digit(total, position):
    mine = digit(position, 4)
    parts = total.reshape(4, -1, total.shape[-1])
    pick = lambda k: lax.dynamic_index_in_dim(parts, mine ^ k, 0, keepdims=False)
    sent = [exchange(pick(k), k * position) for k in (1, 2, 3)]
    return pick(0) + sent[0] + sent[1] + sent[2]


def local(orbitals, potential):
    count, planes, points = orbitals.shape
    every = ("row", "col")
    devices, n_row, n_col = lax.axis_size(every), lax.axis_size("row"), lax.axis_size("col")
    rows = planes * points // LANES
    mine = count // n_col
    scale = 1.0 / (devices * planes * points)
    forward = [(i, i + 1) for i in range(devices - 1)]
    backward = [(j, i) for i, j in forward]

    tiled = tile_view(orbitals).reshape(count * rows, LANES)
    v = tile_view(potential)
    first, last, packed = extract(tiled, v, count, rows, n_col)
    after = lax.ppermute(first, every, backward)
    before = lax.ppermute(last, every, forward)
    received = lax.all_to_all(packed, "col", split_axis=0, concat_axis=0, tiled=True)

    keep, send = gram(tiled, v, after, before, count, rows, scale)
    g = reduce_digit(keep + exchange(send, 1), 32)
    g = reduce_digit(g, 8)
    g, _ = lax.optimization_barrier((g, received))
    g = reduce_digit(g, 2).reshape(planes, 2 * count)

    up = [(i, i + 1) for i in range(n_row - 1)]
    down = [(j, i) for i, j in up]
    first, last = edges_of(received, mine, rows)
    before, after = lax.ppermute(last, "row", up), lax.ppermute(first, "row", down)
    relayed, applied, sides = to_block(received, mine, rows)
    return g[:, :count], g[:, count:], relayed, fix_edges(applied, sides, before, after)


def solution(mesh):
    in_specs = (P(None, ("row", "col"), None), P(("row", "col"), None))
    out_specs = (
        P(("row", "col"), None),
        P(("row", "col"), None),
        P("col", "row", None),
        P("col", "row", None),
    )
    return jax.shard_map(local, mesh=mesh, in_specs=in_specs, out_specs=out_specs, check_vma=False)
```

```python
import functools

import jax
import jax.numpy as jnp
from jax import lax
from jax.experimental import pallas as pl
from jax.experimental.pallas import tpu as pltpu
from jax.sharding import PartitionSpec as P

LANES = 128
NT = (((1,), (1,)), ((), ()))


def tile_view(x):
    *lead, planes, points = x.shape
    tiles = points // LANES
    n = len(lead)
    x = x.reshape(*lead, planes, tiles, LANES)
    x = x.transpose(*range(n), n + 1, n, n + 2)
    return x.reshape(*lead, tiles * planes, LANES)


def split(x):
    high = x.astype(jnp.bfloat16)
    return high, (x - high.astype(jnp.float32)).astype(jnp.bfloat16)


def extract_kernel(count, rows, x_ref, *refs):
    half = rows // 4
    far = 2 * half

    def run(*starts):
        for o in range(count):
            for ref, start in zip(refs, starts):
                ref[pl.ds(o * half, half), :] = x_ref[pl.ds(o * rows + start, half, stride=2), :]

    core = lax.rem(lax.axis_index("col"), 2)
    pl.when(core == 0)(lambda: run(far + 1, 0, 1, far))
    pl.when(core == 1)(lambda: run(0, far + 1, far, 1))


def extract(x, count, rows):
    half = pltpu.VMEM((count * rows // 4, LANES), jnp.float32)
    return pl.pallas_call(
        functools.partial(extract_kernel, count, rows),
        in_specs=[pl.BlockSpec(memory_space=pltpu.VMEM)],
        out_specs=[pl.BlockSpec(memory_space=pltpu.VMEM)] * 4,
        out_shape=[half] * 4,
        compiler_params=pltpu.CompilerParams(vmem_limit_bytes=10 * 2**20),
        cost_estimate=pl.CostEstimate(flops=0, bytes_accessed=count * rows * LANES * 8, transcendentals=0),
    )(x)


def three_passes(a, b):
    a_high, a_low = split(a)
    b_high, b_low = split(b)
    dot = functools.partial(lax.dot_general, dimension_numbers=NT, preferred_element_type=jnp.float32)
    return dot(a_high, b_high) + dot(a_high, b_low) + dot(a_low, b_high)


def gram_kernel(count, rows, x_ref, v_ref, g_ref):
    tiles = rows // 2
    lane = lax.broadcasted_iota(jnp.int32, (count, LANES), 1)

    def load(t, p):
        return x_ref[pl.ds(2 * t + p, count, stride=rows), :]

    def rolled(t, p):
        return pltpu.roll(load(t % tiles, p), LANES - 1, 1)

    step = 4
    with_self = with_low = with_half = None
    now = [rolled(0, p) for p in (0, 1)]
    for begin in range(0, tiles, step):
        xs, bs = [], []
        for t in range(begin, begin + step):
            here = [load(t, p) for p in (0, 1)]
            later = [rolled(t + 1, p) for p in (0, 1)]
            for p in (0, 1):
                beside = jnp.where(lane == LANES - 1, later[p], now[p])
                if p == 0:
                    beside = beside + here[1]
                factor = 1.0 + 0.5 * v_ref[pl.ds(2 * t + p, 1), :]
                xs.append(here[p])
                bs.append(factor * here[p] - 0.5 * beside)
            now = later
        x_high, x_low = split(jnp.concatenate(xs, axis=1))
        b_high, b_low = split(jnp.concatenate(bs, axis=1))
        dot = functools.partial(lax.dot_general, dimension_numbers=NT, preferred_element_type=jnp.float32)
        a = dot(x_high, x_high)
        l = dot(x_high, x_low)
        q = dot(x_high, b_high) + dot(x_high, b_low) + dot(x_low, b_high)
        with_self = a if with_self is None else with_self + a
        with_low = l if with_low is None else with_low + l
        with_half = q if with_half is None else with_half + q
    g_ref[:, :count] = with_self + with_low + with_low.T
    g_ref[:, count:] = with_half


def gram(x, v, count, rows):
    return pl.pallas_call(
        functools.partial(gram_kernel, count, rows),
        out_shape=jax.ShapeDtypeStruct((count, 2 * count), jnp.float32),
        in_specs=[pl.BlockSpec(memory_space=pltpu.VMEM)] * 2,
        out_specs=pl.BlockSpec(memory_space=pltpu.VMEM),
        compiler_params=pltpu.CompilerParams(vmem_limit_bytes=16 * 2**20),
        cost_estimate=pl.CostEstimate(
            flops=400 * count * count * rows * LANES, bytes_accessed=count * rows * LANES * 6, transcendentals=0
        ),
    )(x, v)


def finish_kernel(count, rows, scale, g_ref, by_core_ref, core_ref, by_chip_ref, chip_ref, *refs):
    keep_ref, send_ref, work_ref = refs
    half = rows // 4

    def load(ref):
        return jnp.concatenate([ref[pl.ds(t, count, stride=half), :] for t in range(half)], axis=1)

    beside = three_passes(load(by_core_ref), load(core_ref)) + three_passes(load(by_chip_ref), load(chip_ref))
    with_half = g_ref[:, count:] - 0.5 * beside
    first = g_ref[:, :count] * scale
    second = (with_half + with_half.T) * scale
    blocks = count // LANES
    for m, matrix in enumerate((first, second)):
        for j in range(blocks):
            work_ref[m * blocks + j] = matrix[:, j * LANES : (j + 1) * LANES]
    core = lax.rem(lax.axis_index("col"), 2)
    chips = count // 4
    for ref, which in ((keep_ref, core), (send_ref, 1 - core)):
        for b in (0, 1):
            for j in range(2 * blocks):
                ref[:, pl.ds((b * 2 * blocks + j) * LANES, LANES)] = work_ref.at[j][
                    pl.ds(2 * which + b, chips, stride=4), :
                ]


def finish(g, by_core, from_core, by_chip, from_chip, count, rows, scale):
    part = jax.ShapeDtypeStruct((count // 4, 4 * count), jnp.float32)
    return pl.pallas_call(
        functools.partial(finish_kernel, count, rows, scale),
        out_shape=[part, part],
        in_specs=[pl.BlockSpec(memory_space=pltpu.VMEM)] * 5,
        out_specs=[pl.BlockSpec(memory_space=pltpu.VMEM)] * 2,
        scratch_shapes=[pltpu.VMEM((2 * count // LANES, count, LANES), jnp.float32)],
        compiler_params=pltpu.CompilerParams(vmem_limit_bytes=16 * 2**20),
        cost_estimate=pl.CostEstimate(
            flops=3 * count * count * rows * LANES, bytes_accessed=count * rows * LANES * 4, transcendentals=0
        ),
    )(g, by_core, from_core, by_chip, from_chip)


def edges_kernel(orbitals, rows, low_ref, high_ref, near_ref, far_ref):
    def take(ref, source_ref, start):
        for t in range(rows // 2):
            ref[:, pl.ds(t * LANES, LANES)] = source_ref[0, pl.ds(start + 2 * t, orbitals, stride=rows), :]

    even = lax.rem(lax.axis_index("row"), 2) == 0

    @pl.when(even)
    def _():
        take(near_ref, high_ref, 1)
        take(far_ref, low_ref, 0)

    @pl.when(jnp.logical_not(even))
    def _():
        take(near_ref, low_ref, 0)
        take(far_ref, high_ref, 1)


def edges_of(received, orbitals, rows):
    sources, length, _ = received.shape
    out = jax.ShapeDtypeStruct((orbitals, rows // 2 * LANES), jnp.float32)
    return pl.pallas_call(
        functools.partial(edges_kernel, orbitals, rows),
        grid=(1,),
        in_specs=[
            pl.BlockSpec((1, length, LANES), lambda i: (0, 0, 0)),
            pl.BlockSpec((1, length, LANES), lambda i: (sources - 1, 0, 0)),
        ],
        out_specs=[pl.BlockSpec(out.shape, lambda i: (0, 0))] * 2,
        out_shape=[out, out],
        compiler_params=pltpu.CompilerParams(vmem_limit_bytes=8 * 2**20),
        cost_estimate=pl.CostEstimate(flops=0, bytes_accessed=2**18, transcendentals=0),
    )(received, received)


def block_kernel(sources, block, rows, x_ref, v_own_ref, v1_ref, v2_ref, v3_ref, out_ref, applied_ref, sides_ref, *refs):
    v_scr, v_held_ref, work_ref = refs
    tiles, planes = rows // 2, 2 * sources
    points = tiles * LANES

    def interleaved(flat, start, stride, work):
        for k in range(sources):
            for q in range(0, tiles, 4):
                piece = flat[pl.ds(k * stride + start + 2 * q, 8), :]
                for i in range(4):
                    work[pl.ds(planes * (q + i) + 2 * k, 2), :] = piece[2 * i : 2 * i + 2, :]
        return jnp.concatenate([work[pl.ds(planes * t, planes), :] for t in range(tiles)], axis=1)

    @pl.when(pl.program_id(0) == 0)
    def _():
        column = lax.axis_index("col")
        for b, ref in enumerate((v_own_ref, v1_ref, v2_ref, v3_ref)):
            for a in (0, 1):
                for c in (0, 1):
                    start = ref.shape[0] + (2 * a + c - 4) * rows
                    v_held_ref[column ^ (8 * a + 2 * b + c)] = ref[pl.ds(start, rows), :]
        v_scr[...] = 2.0 + interleaved(v_held_ref.reshape(sources * rows, LANES), 0, rows, work_ref.at[0])

    flat = x_ref.reshape(sources * block * rows, LANES)
    row = lax.broadcasted_iota(jnp.int32, (planes, points), 0)
    for o in range(block):
        psi = interleaved(flat, o * rows, block * rows, work_ref.at[o])
        out_ref[o] = psi
        down = jnp.where(row == 0, 0.0, pltpu.roll(psi, 1, 0))
        up = jnp.where(row == planes - 1, 0.0, pltpu.roll(psi, planes - 1, 0))
        beside = pltpu.roll(psi, 1, 1) + pltpu.roll(psi, points - 1, 1)
        applied = v_scr[...] * psi - 0.5 * (down + up) - 0.5 * beside
        applied_ref[o] = applied
        at = pl.program_id(0) * block + o
        sides_ref[0, at] = applied[:8]
        sides_ref[1, at] = applied[planes - 8 :]


def to_block(received, v_parts, orbitals, rows):
    block, sources = 4, received.shape[0]
    planes, points = 2 * sources, rows // 2 * LANES
    received = received.reshape(sources, orbitals, rows, LANES)
    out = jax.ShapeDtypeStruct((orbitals, planes, points), jnp.float32)
    return pl.pallas_call(
        functools.partial(block_kernel, sources, block, rows),
        grid=(orbitals // block,),
        in_specs=[
            pl.BlockSpec((sources, block, rows, LANES), lambda i: (0, i, 0, 0)),
            *[pl.BlockSpec(part.shape, lambda i: (0, 0)) for part in v_parts],
        ],
        out_specs=[pl.BlockSpec((block, planes, points), lambda i: (i, 0, 0))] * 2
        + [pl.BlockSpec(memory_space=pltpu.VMEM)],
        out_shape=[out, out, jax.ShapeDtypeStruct((2, orbitals, 8, points), jnp.float32)],
        scratch_shapes=[
            pltpu.VMEM((planes, points), jnp.float32),
            pltpu.VMEM((sources, rows, LANES), jnp.float32),
            pltpu.VMEM((block, planes * points // LANES, LANES), jnp.float32),
        ],
        compiler_params=pltpu.CompilerParams(vmem_limit_bytes=24 * 2**20),
        cost_estimate=pl.CostEstimate(flops=0, bytes_accessed=12 * orbitals * planes * points, transcendentals=0),
    )(received, *v_parts)


def fix_kernel(near_ref, far_ref, sides_ref, applied_ref, out_ref, work_ref, sem):
    orbitals, planes, _ = applied_ref.shape

    def run(edge_refs):
        for e, edge_ref in enumerate(edge_refs):
            for o in range(orbitals):
                row = 7 * e
                work_ref[e, o] = sides_ref[e, o]
                work_ref[e, o, pl.ds(row, 1), :] = sides_ref[e, o, pl.ds(row, 1), :] - 0.5 * edge_ref[pl.ds(o, 1), :]

    even = lax.rem(lax.axis_index("row"), 2) == 0
    pl.when(even)(lambda: run((far_ref, near_ref)))
    pl.when(jnp.logical_not(even))(lambda: run((near_ref, far_ref)))
    copies = []
    for e in (0, 1):
        for o in range(orbitals):
            target = out_ref.at[o, pl.ds(e * (planes - 8), 8), :]
            copies.append(pltpu.make_async_copy(work_ref.at[e, o], target, sem.at[e, o]))
            copies[-1].start()
    for copy in copies:
        copy.wait()


def fix_edges(applied, sides, near, far):
    orbitals, _, points = applied.shape
    return pl.pallas_call(
        fix_kernel,
        in_specs=[pl.BlockSpec(memory_space=pltpu.VMEM)] * 3 + [pl.BlockSpec(memory_space=pl.ANY)],
        out_specs=pl.BlockSpec(memory_space=pl.ANY),
        out_shape=jax.ShapeDtypeStruct(applied.shape, jnp.float32),
        input_output_aliases={3: 0},
        scratch_shapes=[
            pltpu.VMEM((2, orbitals, 8, points), jnp.float32),
            pltpu.SemaphoreType.DMA((2, orbitals)),
        ],
        compiler_params=pltpu.CompilerParams(vmem_limit_bytes=12 * 2**20),
        cost_estimate=pl.CostEstimate(flops=0, bytes_accessed=32 * orbitals * points, transcendentals=0),
    )(near, far, sides, applied)


def exchange(x, mask):
    every = ("row", "col")
    return lax.ppermute(x, every, [(i, i ^ mask) for i in range(lax.axis_size(every))])


def digit(position, radix):
    return (lax.axis_index(("row", "col")) // position) % radix


def reduce_digit(total, position):
    mine = digit(position, 4)
    parts = total.reshape(4, -1, total.shape[-1])
    pick = lambda k: lax.dynamic_index_in_dim(parts, mine ^ k, 0, keepdims=False)
    sent = [exchange(pick(k), k * position) for k in (1, 2, 3)]
    return pick(0) + sent[0] + sent[1] + sent[2]


def reduce_z_hi(total):
    parts = total.reshape(2, -1, total.shape[-1])
    mine = digit(16, 2)
    pick = lambda k: lax.dynamic_index_in_dim(parts, mine ^ k, 0, keepdims=False)
    z = lambda i: i // 8 % 4
    pairs = [(i, i + 8 * (3 - 2 * z(i))) for i in range(lax.axis_size(("row", "col")))]
    return pick(0) + lax.ppermute(pick(1), ("row", "col"), pairs)


def reduce_chips(total, v):
    total = total.reshape(8, -1, LANES)
    height = total.shape[1]

    def pick(x, mine, k):
        return lax.dynamic_index_in_dim(x, mine ^ k, 0, keepdims=False).reshape(-1, LANES)

    z, x = digit(8, 2), digit(2, 4)
    pair = total.reshape(2, 4, height, LANES)
    got = exchange(jnp.concatenate([pick(pair, z, 1), v]), 8)
    total = (pick(pair, z, 0) + got[: 4 * height]).reshape(4, height, LANES)
    v = jnp.concatenate([v, got[4 * height :]])
    got = [exchange(jnp.concatenate([pick(total, x, k), v]), 2 * k) for k in (1, 2, 3)]
    return sum([part[:height] for part in got], pick(total, x, 0)), [v, *got]


def local(orbitals, potential):
    count, planes, points = orbitals.shape
    every = ("row", "col")
    devices, n_row, n_col = lax.axis_size(every), lax.axis_size("row"), lax.axis_size("col")
    rows = planes * points // LANES
    mine = count // n_col
    scale = 1.0 / (devices * planes * points)

    tiled = tile_view(orbitals).reshape(count * rows, LANES)
    v = tile_view(potential)
    to_core, to_chip, by_core, by_chip = extract(tiled, count, rows)
    orbitals, to_core, to_chip, v = lax.optimization_barrier((orbitals, to_core, to_chip, v))
    from_core = exchange(to_core, 1)
    from_chip = lax.ppermute(to_chip, every, [(i, (i + 1 ^ 1) - 1) for i in range(1, devices - 1)])
    received = lax.all_to_all(orbitals, "col", split_axis=0, concat_axis=0, tiled=True)
    received = tile_view(received.reshape(n_col, mine, planes, points)).reshape(n_col, mine * rows, LANES)

    g = gram(tiled, v, count, rows)
    keep, send = finish(g, by_core, from_core, by_chip, from_chip, count, rows, scale)
    v = jnp.concatenate([v, exchange(v, 1)])
    g = reduce_digit(keep + exchange(send, 1), 32)
    g = reduce_z_hi(g)
    g, v_parts = reduce_chips(g, v)
    g = g.reshape(planes, 2 * count)

    near, far = edges_of(received, mine, rows)
    near = lax.ppermute(near, "row", [(i, i ^ 1) for i in range(n_row)])
    far = lax.ppermute(far, "row", [(i, (i + 1 ^ 1) - 1) for i in range(1, n_row - 1)])
    relayed, applied, sides = to_block(received, v_parts, mine, rows)
    return g[:, :count], g[:, count:], relayed, fix_edges(applied, sides, near, far)


def solution(mesh):
    in_specs = (P(None, ("row", "col"), None), P(("row", "col"), None))
    out_specs = (
        P(("row", "col"), None),
        P(("row", "col"), None),
        P("col", "row", None),
        P("col", "row", None),
    )
    return jax.shard_map(local, mesh=mesh, in_specs=in_specs, out_specs=out_specs, check_vma=False)
```

```python
import functools

import jax
import jax.numpy as jnp
from jax import lax
from jax.experimental import pallas as pl
from jax.experimental.pallas import tpu as pltpu
from jax.sharding import PartitionSpec as P

LANES = 128
NT = (((1,), (1,)), ((), ()))


def tile_view(x):
    *lead, planes, points = x.shape
    tiles = points // LANES
    n = len(lead)
    x = x.reshape(*lead, planes, tiles, LANES)
    x = x.transpose(*range(n), n + 1, n, n + 2)
    return x.reshape(*lead, tiles * planes, LANES)


def split(x):
    high = x.astype(jnp.bfloat16)
    return high, (x - high.astype(jnp.float32)).astype(jnp.bfloat16)


def cut(count, rows, x_ref, starts, refs):
    half = rows // 4
    for o in range(count):
        for ref, start in zip(refs, starts):
            ref[pl.ds(o * half, half), :] = x_ref[pl.ds(o * rows + start, half, stride=2), :]


def extract_kernel(count, rows, x_ref, *refs):
    core = lax.rem(lax.axis_index("col"), 2)
    pl.when(core == 0)(lambda: cut(count, rows, x_ref, (rows // 2 + 1, 0), refs))
    pl.when(core == 1)(lambda: cut(count, rows, x_ref, (0, rows // 2 + 1), refs))


def extract(x, count, rows):
    half = jax.ShapeDtypeStruct((count * rows // 4, LANES), jnp.float32)
    return pl.pallas_call(
        functools.partial(extract_kernel, count, rows),
        in_specs=[pl.BlockSpec(memory_space=pltpu.VMEM)],
        out_specs=[pl.BlockSpec(memory_space=pltpu.VMEM)] * 2,
        out_shape=[half] * 2,
        compiler_params=pltpu.CompilerParams(vmem_limit_bytes=8 * 2**20),
        cost_estimate=pl.CostEstimate(flops=0, bytes_accessed=count * rows * LANES * 6, transcendentals=0),
    )(x)


def three_passes(a, b):
    a_high, a_low = split(a)
    b_high, b_low = split(b)
    dot = functools.partial(lax.dot_general, dimension_numbers=NT, preferred_element_type=jnp.float32)
    return dot(a_high, b_high) + dot(a_high, b_low) + dot(a_low, b_high)


def gram_kernel(count, rows, x_ref, v_ref, g_ref, by_core_ref, by_chip_ref):
    tiles = rows // 2
    lane = lax.broadcasted_iota(jnp.int32, (count, LANES), 1)

    def load(t, p):
        return x_ref[pl.ds(2 * t + p, count, stride=rows), :]

    def rolled(t, p):
        return pltpu.roll(load(t % tiles, p), LANES - 1, 1)

    step = 4
    with_self = with_low = with_half = None
    now = [rolled(0, p) for p in (0, 1)]
    for begin in range(0, tiles, step):
        xs, bs = [], []
        for t in range(begin, begin + step):
            here = [load(t, p) for p in (0, 1)]
            later = [rolled(t + 1, p) for p in (0, 1)]
            for p in (0, 1):
                beside = jnp.where(lane == LANES - 1, later[p], now[p])
                if p == 0:
                    beside = beside + here[1]
                factor = 1.0 + 0.5 * v_ref[pl.ds(2 * t + p, 1), :]
                xs.append(here[p])
                bs.append(factor * here[p] - 0.5 * beside)
            now = later
        x_high, x_low = split(jnp.concatenate(xs, axis=1))
        b_high, b_low = split(jnp.concatenate(bs, axis=1))
        dot = functools.partial(lax.dot_general, dimension_numbers=NT, preferred_element_type=jnp.float32)
        a = dot(x_high, x_high)
        l = dot(x_high, x_low)
        q = dot(x_high, b_high) + dot(x_high, b_low) + dot(x_low, b_high)
        with_self = a if with_self is None else with_self + a
        with_low = l if with_low is None else with_low + l
        with_half = q if with_half is None else with_half + q
    g_ref[:, :count] = with_self + with_low + with_low.T
    g_ref[:, count:] = with_half
    refs = (by_core_ref, by_chip_ref)
    core = lax.rem(lax.axis_index("col"), 2)
    pl.when(core == 0)(lambda: cut(count, rows, x_ref, (1, rows // 2), refs))
    pl.when(core == 1)(lambda: cut(count, rows, x_ref, (rows // 2, 1), refs))


def gram(x, v, count, rows):
    half = jax.ShapeDtypeStruct((count * rows // 4, LANES), jnp.float32)
    return pl.pallas_call(
        functools.partial(gram_kernel, count, rows),
        out_shape=[jax.ShapeDtypeStruct((count, 2 * count), jnp.float32), half, half],
        in_specs=[pl.BlockSpec(memory_space=pltpu.VMEM)] * 2,
        out_specs=[pl.BlockSpec(memory_space=pltpu.VMEM)] * 3,
        compiler_params=pltpu.CompilerParams(vmem_limit_bytes=16 * 2**20),
        cost_estimate=pl.CostEstimate(
            flops=400 * count * count * rows * LANES, bytes_accessed=count * rows * LANES * 6, transcendentals=0
        ),
    )(x, v)


def finish_kernel(count, rows, scale, g_ref, by_core_ref, core_ref, by_chip_ref, chip_ref, *refs):
    keep_ref, send_ref, work_ref = refs
    half = rows // 4

    def load(ref):
        return jnp.concatenate([ref[pl.ds(t, count, stride=half), :] for t in range(half)], axis=1)

    beside = three_passes(load(by_core_ref), load(core_ref)) + three_passes(load(by_chip_ref), load(chip_ref))
    with_half = g_ref[:, count:] - 0.5 * beside
    first = g_ref[:, :count] * scale
    second = (with_half + with_half.T) * scale
    blocks = count // LANES
    for m, matrix in enumerate((first, second)):
        for j in range(blocks):
            work_ref[m * blocks + j] = matrix[:, j * LANES : (j + 1) * LANES]
    core = lax.rem(lax.axis_index("col"), 2)
    chips = count // 4
    for ref, which in ((keep_ref, core), (send_ref, 1 - core)):
        for b in (0, 1):
            for j in range(2 * blocks):
                ref[:, pl.ds((b * 2 * blocks + j) * LANES, LANES)] = work_ref.at[j][
                    pl.ds(2 * which + b, chips, stride=4), :
                ]


def finish(g, by_core, from_core, by_chip, from_chip, count, rows, scale):
    part = jax.ShapeDtypeStruct((count // 4, 4 * count), jnp.float32)
    return pl.pallas_call(
        functools.partial(finish_kernel, count, rows, scale),
        out_shape=[part, part],
        in_specs=[pl.BlockSpec(memory_space=pltpu.VMEM)] * 5,
        out_specs=[pl.BlockSpec(memory_space=pltpu.VMEM)] * 2,
        scratch_shapes=[pltpu.VMEM((2 * count // LANES, count, LANES), jnp.float32)],
        compiler_params=pltpu.CompilerParams(vmem_limit_bytes=16 * 2**20),
        cost_estimate=pl.CostEstimate(
            flops=3 * count * count * rows * LANES, bytes_accessed=count * rows * LANES * 4, transcendentals=0
        ),
    )(g, by_core, from_core, by_chip, from_chip)


def edges_kernel(orbitals, rows, low_ref, high_ref, near_ref, far_ref):
    def take(ref, source_ref, start):
        for t in range(rows // 2):
            ref[:, pl.ds(t * LANES, LANES)] = source_ref[0, pl.ds(start + 2 * t, orbitals, stride=rows), :]

    even = lax.rem(lax.axis_index("row"), 2) == 0

    @pl.when(even)
    def _():
        take(near_ref, high_ref, 1)
        take(far_ref, low_ref, 0)

    @pl.when(jnp.logical_not(even))
    def _():
        take(near_ref, low_ref, 0)
        take(far_ref, high_ref, 1)


def edges_of(received, orbitals, rows):
    sources, length, _ = received.shape
    out = jax.ShapeDtypeStruct((orbitals, rows // 2 * LANES), jnp.float32)
    return pl.pallas_call(
        functools.partial(edges_kernel, orbitals, rows),
        grid=(1,),
        in_specs=[
            pl.BlockSpec((1, length, LANES), lambda i: (0, 0, 0)),
            pl.BlockSpec((1, length, LANES), lambda i: (sources - 1, 0, 0)),
        ],
        out_specs=[pl.BlockSpec(out.shape, lambda i: (0, 0))] * 2,
        out_shape=[out, out],
        compiler_params=pltpu.CompilerParams(vmem_limit_bytes=8 * 2**20),
        cost_estimate=pl.CostEstimate(flops=0, bytes_accessed=2**18, transcendentals=0),
    )(received, received)


def block_kernel(sources, block, rows, x_ref, v_own_ref, v1_ref, v2_ref, v3_ref, out_ref, applied_ref, sides_ref, *refs):
    v_scr, v_held_ref, work_ref = refs
    tiles, planes = rows // 2, 2 * sources
    points = tiles * LANES

    def interleaved(flat, start, stride, work):
        for k in range(sources):
            for q in range(0, tiles, 4):
                piece = flat[pl.ds(k * stride + start + 2 * q, 8), :]
                for i in range(4):
                    work[pl.ds(planes * (q + i) + 2 * k, 2), :] = piece[2 * i : 2 * i + 2, :]
        return jnp.concatenate([work[pl.ds(planes * t, planes), :] for t in range(tiles)], axis=1)

    @pl.when(pl.program_id(0) == 0)
    def _():
        column = lax.axis_index("col")
        for b, ref in enumerate((v_own_ref, v1_ref, v2_ref, v3_ref)):
            for a in (0, 1):
                for c in (0, 1):
                    start = ref.shape[0] + (2 * c + a - 4) * rows
                    v_held_ref[column ^ (8 * a + 2 * b + c)] = ref[pl.ds(start, rows), :]
        v_scr[...] = 2.0 + interleaved(v_held_ref.reshape(sources * rows, LANES), 0, rows, work_ref.at[0])

    flat = x_ref.reshape(sources * block * rows, LANES)
    row = lax.broadcasted_iota(jnp.int32, (planes, points), 0)
    for o in range(block):
        psi = interleaved(flat, o * rows, block * rows, work_ref.at[o])
        out_ref[o] = psi
        down = jnp.where(row == 0, 0.0, pltpu.roll(psi, 1, 0))
        up = jnp.where(row == planes - 1, 0.0, pltpu.roll(psi, planes - 1, 0))
        beside = pltpu.roll(psi, 1, 1) + pltpu.roll(psi, points - 1, 1)
        applied = v_scr[...] * psi - 0.5 * (down + up) - 0.5 * beside
        applied_ref[o] = applied
        at = pl.program_id(0) * block + o
        sides_ref[0, at] = applied[:8]
        sides_ref[1, at] = applied[planes - 8 :]


def to_block(received, v_parts, orbitals, rows):
    block, sources = 4, received.shape[0]
    planes, points = 2 * sources, rows // 2 * LANES
    received = received.reshape(sources, orbitals, rows, LANES)
    out = jax.ShapeDtypeStruct((orbitals, planes, points), jnp.float32)
    return pl.pallas_call(
        functools.partial(block_kernel, sources, block, rows),
        grid=(orbitals // block,),
        in_specs=[
            pl.BlockSpec((sources, block, rows, LANES), lambda i: (0, i, 0, 0)),
            *[pl.BlockSpec(part.shape, lambda i: (0, 0)) for part in v_parts],
        ],
        out_specs=[pl.BlockSpec((block, planes, points), lambda i: (i, 0, 0))] * 2
        + [pl.BlockSpec(memory_space=pltpu.VMEM)],
        out_shape=[out, out, jax.ShapeDtypeStruct((2, orbitals, 8, points), jnp.float32)],
        scratch_shapes=[
            pltpu.VMEM((planes, points), jnp.float32),
            pltpu.VMEM((sources, rows, LANES), jnp.float32),
            pltpu.VMEM((block, planes * points // LANES, LANES), jnp.float32),
        ],
        compiler_params=pltpu.CompilerParams(vmem_limit_bytes=24 * 2**20),
        cost_estimate=pl.CostEstimate(flops=0, bytes_accessed=12 * orbitals * planes * points, transcendentals=0),
    )(received, *v_parts)


def fix_kernel(near_ref, far_ref, sides_ref, applied_ref, out_ref, work_ref, sem):
    orbitals, planes, _ = applied_ref.shape

    def run(edge_refs):
        for e, edge_ref in enumerate(edge_refs):
            for o in range(orbitals):
                row = 7 * e
                work_ref[e, o] = sides_ref[e, o]
                work_ref[e, o, pl.ds(row, 1), :] = sides_ref[e, o, pl.ds(row, 1), :] - 0.5 * edge_ref[pl.ds(o, 1), :]

    even = lax.rem(lax.axis_index("row"), 2) == 0
    pl.when(even)(lambda: run((far_ref, near_ref)))
    pl.when(jnp.logical_not(even))(lambda: run((near_ref, far_ref)))
    copies = []
    for e in (0, 1):
        for o in range(orbitals):
            target = out_ref.at[o, pl.ds(e * (planes - 8), 8), :]
            copies.append(pltpu.make_async_copy(work_ref.at[e, o], target, sem.at[e, o]))
            copies[-1].start()
    for copy in copies:
        copy.wait()


def fix_edges(applied, sides, near, far):
    orbitals, _, points = applied.shape
    return pl.pallas_call(
        fix_kernel,
        in_specs=[pl.BlockSpec(memory_space=pltpu.VMEM)] * 3 + [pl.BlockSpec(memory_space=pl.ANY)],
        out_specs=pl.BlockSpec(memory_space=pl.ANY),
        out_shape=jax.ShapeDtypeStruct(applied.shape, jnp.float32),
        input_output_aliases={3: 0},
        scratch_shapes=[
            pltpu.VMEM((2, orbitals, 8, points), jnp.float32),
            pltpu.SemaphoreType.DMA((2, orbitals)),
        ],
        compiler_params=pltpu.CompilerParams(vmem_limit_bytes=12 * 2**20),
        cost_estimate=pl.CostEstimate(flops=0, bytes_accessed=32 * orbitals * points, transcendentals=0),
    )(near, far, sides, applied)


def exchange(x, mask):
    every = ("row", "col")
    return lax.ppermute(x, every, [(i, i ^ mask) for i in range(lax.axis_size(every))])


def digit(position, radix):
    return (lax.axis_index(("row", "col")) // position) % radix


def reduce_digit(total, position):
    mine = digit(position, 4)
    parts = total.reshape(4, -1, total.shape[-1])
    pick = lambda k: lax.dynamic_index_in_dim(parts, mine ^ k, 0, keepdims=False)
    sent = [exchange(pick(k), k * position) for k in (1, 2, 3)]
    return pick(0) + sent[0] + sent[1] + sent[2]


def reduce_z_hi(total):
    parts = total.reshape(2, -1, total.shape[-1])
    mine = digit(16, 2)
    pick = lambda k: lax.dynamic_index_in_dim(parts, mine ^ k, 0, keepdims=False)
    z = lambda i: i // 8 % 4
    pairs = [(i, i + 8 * (3 - 2 * z(i))) for i in range(lax.axis_size(("row", "col")))]
    return pick(0) + lax.ppermute(pick(1), ("row", "col"), pairs)


def reduce_x(total, v):
    total = total.reshape(2, 4, -1, LANES)
    x = digit(2, 4)
    pick = lambda k: lax.dynamic_index_in_dim(total, x ^ k, 1, keepdims=False).reshape(-1, LANES)
    got = [exchange(jnp.concatenate([pick(k), v]), 2 * k) for k in (1, 2, 3)]
    height = got[0].shape[0] - v.shape[0]
    return sum([part[:height] for part in got], pick(0)), [v, *got]


def reduce_z_lo(total):
    total = total.reshape(2, -1, LANES)
    z = digit(8, 2)
    pick = lambda k: lax.dynamic_index_in_dim(total, z ^ k, 0, keepdims=False)
    return pick(0) + exchange(pick(1), 8)


def local(orbitals, potential):
    count, planes, points = orbitals.shape
    every = ("row", "col")
    devices, n_row, n_col = lax.axis_size(every), lax.axis_size("row"), lax.axis_size("col")
    rows = planes * points // LANES
    mine = count // n_col
    scale = 1.0 / (devices * planes * points)

    tiled = tile_view(orbitals).reshape(count * rows, LANES)
    v = tile_view(potential)
    v_z = jnp.concatenate([v, exchange(v, 8)])
    to_core, to_chip = extract(tiled, count, rows)
    orbitals, to_core, to_chip, v, v_z = lax.optimization_barrier((orbitals, to_core, to_chip, v, v_z))
    from_core = exchange(to_core, 1)
    from_chip = lax.ppermute(to_chip, every, [(i, (i + 1 ^ 1) - 1) for i in range(1, devices - 1)])
    received = lax.all_to_all(orbitals, "col", split_axis=0, concat_axis=0, tiled=True)
    received = tile_view(received.reshape(n_col, mine, planes, points)).reshape(n_col, mine * rows, LANES)

    g, by_core, by_chip = gram(tiled, v, count, rows)
    keep, send = finish(g, by_core, from_core, by_chip, from_chip, count, rows, scale)
    v_x = jnp.concatenate([v_z, exchange(v_z, 1)])
    g = reduce_digit(keep + exchange(send, 1), 32)
    g = reduce_z_hi(g)
    g, v_parts = reduce_x(g, v_x)

    near, far = edges_of(received, mine, rows)
    g, near, far = lax.optimization_barrier((g, near, far))
    near = lax.ppermute(near, "row", [(i, i ^ 1) for i in range(n_row)])
    far = lax.ppermute(far, "row", [(i, (i + 1 ^ 1) - 1) for i in range(1, n_row - 1)])
    relayed, applied, sides = to_block(received, v_parts, mine, rows)
    g = reduce_z_lo(g).reshape(planes, 2 * count)
    return g[:, :count], g[:, count:], relayed, fix_edges(applied, sides, near, far)


def solution(mesh):
    in_specs = (P(None, ("row", "col"), None), P(("row", "col"), None))
    out_specs = (
        P(("row", "col"), None),
        P(("row", "col"), None),
        P("col", "row", None),
        P("col", "row", None),
    )
    return jax.shard_map(local, mesh=mesh, in_specs=in_specs, out_specs=out_specs, check_vma=False)
```

```python
import functools

import jax
import jax.numpy as jnp
from jax import lax
from jax.experimental import pallas as pl
from jax.experimental.pallas import tpu as pltpu
from jax.sharding import PartitionSpec as P

LANES = 128
NT = (((1,), (1,)), ((), ()))


def tile_view(x):
    *lead, planes, points = x.shape
    tiles = points // LANES
    n = len(lead)
    x = x.reshape(*lead, planes, tiles, LANES)
    x = x.transpose(*range(n), n + 1, n, n + 2)
    return x.reshape(*lead, tiles * planes, LANES)


def split(x):
    high = x.astype(jnp.bfloat16)
    return high, (x - high.astype(jnp.float32)).astype(jnp.bfloat16)


def cut(count, rows, x_ref, starts, refs):
    half = rows // 4
    for o in range(count):
        for ref, start in zip(refs, starts):
            ref[pl.ds(o * half, half), :] = x_ref[pl.ds(o * rows + start, half, stride=2), :]


def extract_kernel(count, rows, x_ref, *refs):
    core = lax.rem(lax.axis_index("col"), 2)
    pl.when(core == 0)(lambda: cut(count, rows, x_ref, (rows // 2 + 1, 0), refs))
    pl.when(core == 1)(lambda: cut(count, rows, x_ref, (0, rows // 2 + 1), refs))


def extract(x, count, rows):
    half = jax.ShapeDtypeStruct((count * rows // 4, LANES), jnp.float32)
    return pl.pallas_call(
        functools.partial(extract_kernel, count, rows),
        in_specs=[pl.BlockSpec(memory_space=pltpu.VMEM)],
        out_specs=[pl.BlockSpec(memory_space=pltpu.VMEM)] * 2,
        out_shape=[half] * 2,
        compiler_params=pltpu.CompilerParams(vmem_limit_bytes=8 * 2**20),
        cost_estimate=pl.CostEstimate(flops=0, bytes_accessed=count * rows * LANES * 6, transcendentals=0),
    )(x)


def three_passes(a, b):
    a_high, a_low = split(a)
    b_high, b_low = split(b)
    dot = functools.partial(lax.dot_general, dimension_numbers=NT, preferred_element_type=jnp.float32)
    return dot(a_high, b_high) + dot(a_high, b_low) + dot(a_low, b_high)


def gram_kernel(count, rows, x_ref, v_ref, g_ref, by_core_ref, by_chip_ref):
    tiles = rows // 2
    lane = lax.broadcasted_iota(jnp.int32, (count, LANES), 1)

    def load(t, p):
        return x_ref[pl.ds(2 * t + p, count, stride=rows), :]

    def rolled(t, p):
        return pltpu.roll(load(t % tiles, p), LANES - 1, 1)

    step = 4
    with_self = with_low = with_half = None
    now = [rolled(0, p) for p in (0, 1)]
    for begin in range(0, tiles, step):
        xs, bs = [], []
        for t in range(begin, begin + step):
            here = [load(t, p) for p in (0, 1)]
            later = [rolled(t + 1, p) for p in (0, 1)]
            for p in (0, 1):
                beside = jnp.where(lane == LANES - 1, later[p], now[p])
                if p == 0:
                    beside = beside + here[1]
                factor = 1.0 + 0.5 * v_ref[pl.ds(2 * t + p, 1), :]
                xs.append(here[p])
                bs.append(factor * here[p] - 0.5 * beside)
            now = later
        x_high, x_low = split(jnp.concatenate(xs, axis=1))
        b_high, b_low = split(jnp.concatenate(bs, axis=1))
        dot = functools.partial(lax.dot_general, dimension_numbers=NT, preferred_element_type=jnp.float32)
        a = dot(x_high, x_high)
        l = dot(x_high, x_low)
        q = dot(x_high, b_high) + dot(x_high, b_low) + dot(x_low, b_high)
        with_self = a if with_self is None else with_self + a
        with_low = l if with_low is None else with_low + l
        with_half = q if with_half is None else with_half + q
    g_ref[:, :count] = with_self + with_low + with_low.T
    g_ref[:, count:] = with_half
    refs = (by_core_ref, by_chip_ref)
    core = lax.rem(lax.axis_index("col"), 2)
    pl.when(core == 0)(lambda: cut(count, rows, x_ref, (1, rows // 2), refs))
    pl.when(core == 1)(lambda: cut(count, rows, x_ref, (rows // 2, 1), refs))


def gram(x, v, count, rows):
    half = jax.ShapeDtypeStruct((count * rows // 4, LANES), jnp.float32)
    return pl.pallas_call(
        functools.partial(gram_kernel, count, rows),
        out_shape=[jax.ShapeDtypeStruct((count, 2 * count), jnp.float32), half, half],
        in_specs=[pl.BlockSpec(memory_space=pltpu.VMEM)] * 2,
        out_specs=[pl.BlockSpec(memory_space=pltpu.VMEM)] * 3,
        compiler_params=pltpu.CompilerParams(vmem_limit_bytes=16 * 2**20),
        cost_estimate=pl.CostEstimate(
            flops=400 * count * count * rows * LANES, bytes_accessed=count * rows * LANES * 6, transcendentals=0
        ),
    )(x, v)


def finish_kernel(count, rows, scale, g_ref, by_core_ref, core_ref, by_chip_ref, chip_ref, *refs):
    keep_ref, send_ref, work_ref = refs
    half = rows // 4

    def load(ref):
        return jnp.concatenate([ref[pl.ds(t, count, stride=half), :] for t in range(half)], axis=1)

    beside = three_passes(load(by_core_ref), load(core_ref)) + three_passes(load(by_chip_ref), load(chip_ref))
    with_half = g_ref[:, count:] - 0.5 * beside
    first = g_ref[:, :count] * scale
    second = (with_half + with_half.T) * scale
    blocks = count // LANES
    for m, matrix in enumerate((first, second)):
        for j in range(blocks):
            work_ref[m * blocks + j] = matrix[:, j * LANES : (j + 1) * LANES]
    core = lax.rem(lax.axis_index("col"), 2)
    chips = count // 4
    for ref, which in ((keep_ref, core), (send_ref, 1 - core)):
        for b in (0, 1):
            for j in range(2 * blocks):
                ref[:, pl.ds((b * 2 * blocks + j) * LANES, LANES)] = work_ref.at[j][
                    pl.ds(2 * which + b, chips, stride=4), :
                ]


def finish(g, by_core, from_core, by_chip, from_chip, count, rows, scale):
    part = jax.ShapeDtypeStruct((count // 4, 4 * count), jnp.float32)
    return pl.pallas_call(
        functools.partial(finish_kernel, count, rows, scale),
        out_shape=[part, part],
        in_specs=[pl.BlockSpec(memory_space=pltpu.VMEM)] * 5,
        out_specs=[pl.BlockSpec(memory_space=pltpu.VMEM)] * 2,
        scratch_shapes=[pltpu.VMEM((2 * count // LANES, count, LANES), jnp.float32)],
        compiler_params=pltpu.CompilerParams(vmem_limit_bytes=16 * 2**20),
        cost_estimate=pl.CostEstimate(
            flops=3 * count * count * rows * LANES, bytes_accessed=count * rows * LANES * 4, transcendentals=0
        ),
    )(g, by_core, from_core, by_chip, from_chip)


def edges_kernel(orbitals, rows, low_ref, high_ref, near_ref, far_ref):
    def take(ref, source_ref, start):
        for t in range(rows // 2):
            ref[:, pl.ds(t * LANES, LANES)] = source_ref[0, pl.ds(start + 2 * t, orbitals, stride=rows), :]

    even = lax.rem(lax.axis_index("row"), 2) == 0

    @pl.when(even)
    def _():
        take(near_ref, high_ref, 1)
        take(far_ref, low_ref, 0)

    @pl.when(jnp.logical_not(even))
    def _():
        take(near_ref, low_ref, 0)
        take(far_ref, high_ref, 1)


def edges_of(received, orbitals, rows):
    sources, length, _ = received.shape
    out = jax.ShapeDtypeStruct((orbitals, rows // 2 * LANES), jnp.float32)
    return pl.pallas_call(
        functools.partial(edges_kernel, orbitals, rows),
        grid=(1,),
        in_specs=[
            pl.BlockSpec((1, length, LANES), lambda i: (0, 0, 0)),
            pl.BlockSpec((1, length, LANES), lambda i: (sources - 1, 0, 0)),
        ],
        out_specs=[pl.BlockSpec(out.shape, lambda i: (0, 0))] * 2,
        out_shape=[out, out],
        compiler_params=pltpu.CompilerParams(vmem_limit_bytes=8 * 2**20),
        cost_estimate=pl.CostEstimate(flops=0, bytes_accessed=2**18, transcendentals=0),
    )(received, received)


def block_kernel(sources, block, rows, x_ref, v_own_ref, v1_ref, v2_ref, v3_ref, out_ref, applied_ref, sides_ref, *refs):
    v_scr, v_held_ref, work_ref = refs
    tiles, planes = rows // 2, 2 * sources
    points = tiles * LANES

    def interleaved(flat, start, stride, work):
        for k in range(sources):
            for q in range(0, tiles, 4):
                piece = flat[pl.ds(k * stride + start + 2 * q, 8), :]
                for i in range(4):
                    work[pl.ds(planes * (q + i) + 2 * k, 2), :] = piece[2 * i : 2 * i + 2, :]
        return jnp.concatenate([work[pl.ds(planes * t, planes), :] for t in range(tiles)], axis=1)

    @pl.when(pl.program_id(0) == 0)
    def _():
        column = lax.axis_index("col")
        for b, ref in enumerate((v_own_ref, v1_ref, v2_ref, v3_ref)):
            for a in (0, 1):
                for c in (0, 1):
                    start = ref.shape[0] + (2 * c + a - 4) * rows
                    v_held_ref[column ^ (8 * a + 2 * b + c)] = ref[pl.ds(start, rows), :]
        v_scr[...] = 2.0 + interleaved(v_held_ref.reshape(sources * rows, LANES), 0, rows, work_ref.at[0])

    flat = x_ref.reshape(sources * block * rows, LANES)
    row = lax.broadcasted_iota(jnp.int32, (planes, points), 0)
    for o in range(block):
        psi = interleaved(flat, o * rows, block * rows, work_ref.at[o])
        out_ref[o] = psi
        down = jnp.where(row == 0, 0.0, pltpu.roll(psi, 1, 0))
        up = jnp.where(row == planes - 1, 0.0, pltpu.roll(psi, planes - 1, 0))
        beside = pltpu.roll(psi, 1, 1) + pltpu.roll(psi, points - 1, 1)
        applied = v_scr[...] * psi - 0.5 * (down + up) - 0.5 * beside
        applied_ref[o] = applied
        at = pl.program_id(0) * block + o
        sides_ref[0, at] = applied[:8]
        sides_ref[1, at] = applied[planes - 8 :]


def to_block(received, v_parts, orbitals, rows):
    block, sources = 4, received.shape[0]
    planes, points = 2 * sources, rows // 2 * LANES
    received = received.reshape(sources, orbitals, rows, LANES)
    out = jax.ShapeDtypeStruct((orbitals, planes, points), jnp.float32)
    return pl.pallas_call(
        functools.partial(block_kernel, sources, block, rows),
        grid=(orbitals // block,),
        in_specs=[
            pl.BlockSpec((sources, block, rows, LANES), lambda i: (0, i, 0, 0)),
            *[pl.BlockSpec(part.shape, lambda i: (0, 0)) for part in v_parts],
        ],
        out_specs=[pl.BlockSpec((block, planes, points), lambda i: (i, 0, 0))] * 2
        + [pl.BlockSpec(memory_space=pltpu.VMEM)],
        out_shape=[out, out, jax.ShapeDtypeStruct((2, orbitals, 8, points), jnp.float32)],
        scratch_shapes=[
            pltpu.VMEM((planes, points), jnp.float32),
            pltpu.VMEM((sources, rows, LANES), jnp.float32),
            pltpu.VMEM((block, planes * points // LANES, LANES), jnp.float32),
        ],
        compiler_params=pltpu.CompilerParams(vmem_limit_bytes=24 * 2**20),
        cost_estimate=pl.CostEstimate(flops=0, bytes_accessed=12 * orbitals * planes * points, transcendentals=0),
    )(received, *v_parts)


def fix_kernel(near_ref, far_ref, sides_ref, applied_ref, out_ref, work_ref, sem):
    orbitals, planes, _ = applied_ref.shape

    def run(edge_refs):
        for e, edge_ref in enumerate(edge_refs):
            for o in range(orbitals):
                row = 7 * e
                work_ref[e, o] = sides_ref[e, o]
                work_ref[e, o, pl.ds(row, 1), :] = sides_ref[e, o, pl.ds(row, 1), :] - 0.5 * edge_ref[pl.ds(o, 1), :]

    even = lax.rem(lax.axis_index("row"), 2) == 0
    pl.when(even)(lambda: run((far_ref, near_ref)))
    pl.when(jnp.logical_not(even))(lambda: run((near_ref, far_ref)))
    copies = []
    for e in (0, 1):
        for o in range(orbitals):
            target = out_ref.at[o, pl.ds(e * (planes - 8), 8), :]
            copies.append(pltpu.make_async_copy(work_ref.at[e, o], target, sem.at[e, o]))
            copies[-1].start()
    for copy in copies:
        copy.wait()


def fix_edges(applied, sides, near, far):
    orbitals, _, points = applied.shape
    return pl.pallas_call(
        fix_kernel,
        in_specs=[pl.BlockSpec(memory_space=pltpu.VMEM)] * 3 + [pl.BlockSpec(memory_space=pl.ANY)],
        out_specs=pl.BlockSpec(memory_space=pl.ANY),
        out_shape=jax.ShapeDtypeStruct(applied.shape, jnp.float32),
        input_output_aliases={3: 0},
        scratch_shapes=[
            pltpu.VMEM((2, orbitals, 8, points), jnp.float32),
            pltpu.SemaphoreType.DMA((2, orbitals)),
        ],
        compiler_params=pltpu.CompilerParams(vmem_limit_bytes=12 * 2**20),
        cost_estimate=pl.CostEstimate(flops=0, bytes_accessed=32 * orbitals * points, transcendentals=0),
    )(near, far, sides, applied)


def exchange(x, mask):
    every = ("row", "col")
    return lax.ppermute(x, every, [(i, i ^ mask) for i in range(lax.axis_size(every))])


def digit(position, radix):
    return (lax.axis_index(("row", "col")) // position) % radix


def reduce_digit(total, position):
    mine = digit(position, 4)
    parts = total.reshape(4, -1, total.shape[-1])
    pick = lambda k: lax.dynamic_index_in_dim(parts, mine ^ k, 0, keepdims=False)
    sent = [exchange(pick(k), k * position) for k in (1, 2, 3)]
    return pick(0) + sent[0] + sent[1] + sent[2]


def reduce_z_hi(total):
    parts = total.reshape(2, -1, total.shape[-1])
    mine = digit(16, 2)
    pick = lambda k: lax.dynamic_index_in_dim(parts, mine ^ k, 0, keepdims=False)
    z = lambda i: i // 8 % 4
    pairs = [(i, i + 8 * (3 - 2 * z(i))) for i in range(lax.axis_size(("row", "col")))]
    return pick(0) + lax.ppermute(pick(1), ("row", "col"), pairs)


def reduce_x(total, v):
    total = total.reshape(2, 4, -1, LANES)
    x = digit(2, 4)
    pick = lambda k: lax.dynamic_index_in_dim(total, x ^ k, 1, keepdims=False).reshape(-1, LANES)
    got = [exchange(jnp.concatenate([pick(k), v]), 2 * k) for k in (1, 2, 3)]
    height = got[0].shape[0] - v.shape[0]
    return sum([part[:height] for part in got], pick(0)), [v, *got]


def reduce_z_lo(total):
    total = total.reshape(2, -1, LANES)
    z = digit(8, 2)
    pick = lambda k: lax.dynamic_index_in_dim(total, z ^ k, 0, keepdims=False)
    return pick(0) + exchange(pick(1), 8)


def local(orbitals, potential):
    count, planes, points = orbitals.shape
    every = ("row", "col")
    devices, n_row, n_col = lax.axis_size(every), lax.axis_size("row"), lax.axis_size("col")
    rows = planes * points // LANES
    mine = count // n_col
    scale = 1.0 / (devices * planes * points)

    tiled = tile_view(orbitals).reshape(count * rows, LANES)
    v = tile_view(potential)
    to_core, to_chip = extract(tiled, count, rows)
    orbitals, to_core, to_chip, v = lax.optimization_barrier((orbitals, to_core, to_chip, v))
    v_z = jnp.concatenate([v, exchange(v, 8)])
    from_core = exchange(to_core, 1)
    from_chip = lax.ppermute(to_chip, every, [(i, (i + 1 ^ 1) - 1) for i in range(1, devices - 1)])
    received = lax.all_to_all(orbitals, "col", split_axis=0, concat_axis=0, tiled=True)
    received = tile_view(received.reshape(n_col, mine, planes, points)).reshape(n_col, mine * rows, LANES)

    g, by_core, by_chip = gram(tiled, v, count, rows)
    keep, send = finish(g, by_core, from_core, by_chip, from_chip, count, rows, scale)
    v_x = jnp.concatenate([v_z, exchange(v_z, 1)])
    g = reduce_digit(keep + exchange(send, 1), 32)
    g = reduce_z_hi(g)
    g, v_parts = reduce_x(g, v_x)

    near, far = edges_of(received, mine, rows)
    g, near, far = lax.optimization_barrier((g, near, far))
    near = lax.ppermute(near, "row", [(i, i ^ 1) for i in range(n_row)])
    far = lax.ppermute(far, "row", [(i, (i + 1 ^ 1) - 1) for i in range(1, n_row - 1)])
    relayed, applied, sides = to_block(received, v_parts, mine, rows)
    g = reduce_z_lo(g).reshape(planes, 2 * count)
    return g[:, :count], g[:, count:], relayed, fix_edges(applied, sides, near, far)


def solution(mesh):
    in_specs = (P(None, ("row", "col"), None), P(("row", "col"), None))
    out_specs = (
        P(("row", "col"), None),
        P(("row", "col"), None),
        P("col", "row", None),
        P("col", "row", None),
    )
    return jax.shard_map(local, mesh=mesh, in_specs=in_specs, out_specs=out_specs, check_vma=False)
```

```python
import functools

import jax
import jax.numpy as jnp
from jax import lax
from jax.experimental import pallas as pl
from jax.experimental.pallas import tpu as pltpu
from jax.sharding import PartitionSpec as P

LANES = 128
NT = (((1,), (1,)), ((), ()))


def tile_view(x):
    *lead, planes, points = x.shape
    tiles = points // LANES
    n = len(lead)
    x = x.reshape(*lead, planes, tiles, LANES)
    x = x.transpose(*range(n), n + 1, n, n + 2)
    return x.reshape(*lead, tiles * planes, LANES)


def split(x):
    high = x.astype(jnp.bfloat16)
    return high, (x - high.astype(jnp.float32)).astype(jnp.bfloat16)


def cut(count, rows, x_ref, starts, refs):
    half = rows // 4
    for o in range(count):
        for ref, start in zip(refs, starts):
            ref[pl.ds(o * half, half), :] = x_ref[pl.ds(o * rows + start, half, stride=2), :]


def extract_kernel(count, rows, x_ref, *refs):
    core = lax.rem(lax.axis_index("col"), 2)
    pl.when(core == 0)(lambda: cut(count, rows, x_ref, (rows // 2 + 1, 0), refs))
    pl.when(core == 1)(lambda: cut(count, rows, x_ref, (0, rows // 2 + 1), refs))


def extract(x, count, rows):
    half = jax.ShapeDtypeStruct((count * rows // 4, LANES), jnp.float32)
    return pl.pallas_call(
        functools.partial(extract_kernel, count, rows),
        in_specs=[pl.BlockSpec(memory_space=pltpu.VMEM)],
        out_specs=[pl.BlockSpec(memory_space=pltpu.VMEM)] * 2,
        out_shape=[half] * 2,
        compiler_params=pltpu.CompilerParams(vmem_limit_bytes=8 * 2**20),
        cost_estimate=pl.CostEstimate(flops=0, bytes_accessed=count * rows * LANES * 6, transcendentals=0),
    )(x)


def three_passes(a, b):
    a_high, a_low = split(a)
    b_high, b_low = split(b)
    dot = functools.partial(lax.dot_general, dimension_numbers=NT, preferred_element_type=jnp.float32)
    return dot(a_high, b_high) + dot(a_high, b_low) + dot(a_low, b_high)


def gram_kernel(count, rows, x_ref, v_ref, g_ref, by_core_ref, by_chip_ref):
    tiles = rows // 2
    lane = lax.broadcasted_iota(jnp.int32, (count, LANES), 1)

    def load(t, p):
        return x_ref[pl.ds(2 * t + p, count, stride=rows), :]

    def rolled(t, p):
        return pltpu.roll(load(t % tiles, p), LANES - 1, 1)

    step = 4
    with_self = with_low = with_half = None
    now = [rolled(0, p) for p in (0, 1)]
    for begin in range(0, tiles, step):
        xs, bs = [], []
        for t in range(begin, begin + step):
            here = [load(t, p) for p in (0, 1)]
            later = [rolled(t + 1, p) for p in (0, 1)]
            for p in (0, 1):
                beside = jnp.where(lane == LANES - 1, later[p], now[p])
                if p == 0:
                    beside = beside + here[1]
                factor = 1.0 + 0.5 * v_ref[pl.ds(2 * t + p, 1), :]
                xs.append(here[p])
                bs.append(factor * here[p] - 0.5 * beside)
            now = later
        x_high, x_low = split(jnp.concatenate(xs, axis=1))
        b_high, b_low = split(jnp.concatenate(bs, axis=1))
        dot = functools.partial(lax.dot_general, dimension_numbers=NT, preferred_element_type=jnp.float32)
        a = dot(x_high, x_high)
        l = dot(x_high, x_low)
        q = dot(x_high, b_high) + dot(x_high, b_low) + dot(x_low, b_high)
        with_self = a if with_self is None else with_self + a
        with_low = l if with_low is None else with_low + l
        with_half = q if with_half is None else with_half + q
    g_ref[:, :count] = with_self + with_low + with_low.T
    g_ref[:, count:] = with_half
    refs = (by_core_ref, by_chip_ref)
    core = lax.rem(lax.axis_index("col"), 2)
    pl.when(core == 0)(lambda: cut(count, rows, x_ref, (1, rows // 2), refs))
    pl.when(core == 1)(lambda: cut(count, rows, x_ref, (rows // 2, 1), refs))


def gram(x, v, count, rows):
    half = jax.ShapeDtypeStruct((count * rows // 4, LANES), jnp.float32)
    return pl.pallas_call(
        functools.partial(gram_kernel, count, rows),
        out_shape=[jax.ShapeDtypeStruct((count, 2 * count), jnp.float32), half, half],
        in_specs=[pl.BlockSpec(memory_space=pltpu.VMEM)] * 2,
        out_specs=[pl.BlockSpec(memory_space=pltpu.VMEM)] * 3,
        compiler_params=pltpu.CompilerParams(vmem_limit_bytes=16 * 2**20),
        cost_estimate=pl.CostEstimate(
            flops=400 * count * count * rows * LANES, bytes_accessed=count * rows * LANES * 6, transcendentals=0
        ),
    )(x, v)


def finish_kernel(count, rows, scale, g_ref, by_core_ref, core_ref, by_chip_ref, chip_ref, *refs):
    keep_ref, send_ref, work_ref = refs
    half = rows // 4

    def load(ref):
        return jnp.concatenate([ref[pl.ds(t, count, stride=half), :] for t in range(half)], axis=1)

    beside = three_passes(load(by_core_ref), load(core_ref)) + three_passes(load(by_chip_ref), load(chip_ref))
    with_half = g_ref[:, count:] - 0.5 * beside
    first = g_ref[:, :count] * scale
    second = (with_half + with_half.T) * scale
    blocks = count // LANES
    for m, matrix in enumerate((first, second)):
        for j in range(blocks):
            work_ref[m * blocks + j] = matrix[:, j * LANES : (j + 1) * LANES]
    core = lax.rem(lax.axis_index("col"), 2)
    chips = count // 4
    for ref, which in ((keep_ref, core), (send_ref, 1 - core)):
        for b in (0, 1):
            for j in range(2 * blocks):
                ref[:, pl.ds((b * 2 * blocks + j) * LANES, LANES)] = work_ref.at[j][
                    pl.ds(2 * which + b, chips, stride=4), :
                ]


def finish(g, by_core, from_core, by_chip, from_chip, count, rows, scale):
    part = jax.ShapeDtypeStruct((count // 4, 4 * count), jnp.float32)
    return pl.pallas_call(
        functools.partial(finish_kernel, count, rows, scale),
        out_shape=[part, part],
        in_specs=[pl.BlockSpec(memory_space=pltpu.VMEM)] * 5,
        out_specs=[pl.BlockSpec(memory_space=pltpu.VMEM)] * 2,
        scratch_shapes=[pltpu.VMEM((2 * count // LANES, count, LANES), jnp.float32)],
        compiler_params=pltpu.CompilerParams(vmem_limit_bytes=16 * 2**20),
        cost_estimate=pl.CostEstimate(
            flops=3 * count * count * rows * LANES, bytes_accessed=count * rows * LANES * 4, transcendentals=0
        ),
    )(g, by_core, from_core, by_chip, from_chip)


def edges_kernel(orbitals, rows, low_ref, high_ref, near_ref, far_ref):
    def take(ref, source_ref, start):
        for t in range(rows // 2):
            ref[:, pl.ds(t * LANES, LANES)] = source_ref[0, pl.ds(start + 2 * t, orbitals, stride=rows), :]

    even = lax.rem(lax.axis_index("row"), 2) == 0

    @pl.when(even)
    def _():
        take(near_ref, high_ref, 1)
        take(far_ref, low_ref, 0)

    @pl.when(jnp.logical_not(even))
    def _():
        take(near_ref, low_ref, 0)
        take(far_ref, high_ref, 1)


def edges_of(received, orbitals, rows):
    sources, length, _ = received.shape
    out = jax.ShapeDtypeStruct((orbitals, rows // 2 * LANES), jnp.float32)
    return pl.pallas_call(
        functools.partial(edges_kernel, orbitals, rows),
        grid=(1,),
        in_specs=[
            pl.BlockSpec((1, length, LANES), lambda i: (0, 0, 0)),
            pl.BlockSpec((1, length, LANES), lambda i: (sources - 1, 0, 0)),
        ],
        out_specs=[pl.BlockSpec(out.shape, lambda i: (0, 0))] * 2,
        out_shape=[out, out],
        compiler_params=pltpu.CompilerParams(vmem_limit_bytes=8 * 2**20),
        cost_estimate=pl.CostEstimate(flops=0, bytes_accessed=2**18, transcendentals=0),
    )(received, received)


def block_kernel(sources, block, rows, x_ref, v_own_ref, v1_ref, v2_ref, v3_ref, out_ref, applied_ref, sides_ref, *refs):
    v_scr, v_held_ref, work_ref = refs
    tiles, planes = rows // 2, 2 * sources
    points = tiles * LANES

    def interleaved(flat, start, stride, work):
        for k in range(sources):
            for q in range(0, tiles, 4):
                piece = flat[pl.ds(k * stride + start + 2 * q, 8), :]
                for i in range(4):
                    work[pl.ds(planes * (q + i) + 2 * k, 2), :] = piece[2 * i : 2 * i + 2, :]
        return jnp.concatenate([work[pl.ds(planes * t, planes), :] for t in range(tiles)], axis=1)

    @pl.when(pl.program_id(0) == 0)
    def _():
        column = lax.axis_index("col")
        for b, ref in enumerate((v_own_ref, v1_ref, v2_ref, v3_ref)):
            for a in (0, 1):
                for c in (0, 1):
                    start = ref.shape[0] + (2 * c + a - 4) * rows
                    v_held_ref[column ^ (8 * a + 2 * b + c)] = ref[pl.ds(start, rows), :]
        v_scr[...] = 2.0 + interleaved(v_held_ref.reshape(sources * rows, LANES), 0, rows, work_ref.at[0])

    flat = x_ref.reshape(sources * block * rows, LANES)
    row = lax.broadcasted_iota(jnp.int32, (planes, points), 0)
    for o in range(block):
        psi = interleaved(flat, o * rows, block * rows, work_ref.at[o])
        out_ref[o] = psi
        down = jnp.where(row == 0, 0.0, pltpu.roll(psi, 1, 0))
        up = jnp.where(row == planes - 1, 0.0, pltpu.roll(psi, planes - 1, 0))
        beside = pltpu.roll(psi, 1, 1) + pltpu.roll(psi, points - 1, 1)
        applied = v_scr[...] * psi - 0.5 * (down + up) - 0.5 * beside
        applied_ref[o] = applied
        at = pl.program_id(0) * block + o
        sides_ref[0, at] = applied[:8]
        sides_ref[1, at] = applied[planes - 8 :]


def to_block(received, v_parts, orbitals, rows):
    block, sources = 4, received.shape[0]
    planes, points = 2 * sources, rows // 2 * LANES
    received = received.reshape(sources, orbitals, rows, LANES)
    out = jax.ShapeDtypeStruct((orbitals, planes, points), jnp.float32)
    return pl.pallas_call(
        functools.partial(block_kernel, sources, block, rows),
        grid=(orbitals // block,),
        in_specs=[
            pl.BlockSpec((sources, block, rows, LANES), lambda i: (0, i, 0, 0)),
            *[pl.BlockSpec(part.shape, lambda i: (0, 0)) for part in v_parts],
        ],
        out_specs=[pl.BlockSpec((block, planes, points), lambda i: (i, 0, 0))] * 2
        + [pl.BlockSpec(memory_space=pltpu.VMEM)],
        out_shape=[out, out, jax.ShapeDtypeStruct((2, orbitals, 8, points), jnp.float32)],
        scratch_shapes=[
            pltpu.VMEM((planes, points), jnp.float32),
            pltpu.VMEM((sources, rows, LANES), jnp.float32),
            pltpu.VMEM((block, planes * points // LANES, LANES), jnp.float32),
        ],
        compiler_params=pltpu.CompilerParams(vmem_limit_bytes=24 * 2**20),
        cost_estimate=pl.CostEstimate(flops=0, bytes_accessed=12 * orbitals * planes * points, transcendentals=0),
    )(received, *v_parts)


def fix_kernel(near_ref, far_ref, sides_ref, applied_ref, out_ref, work_ref, sem):
    orbitals, planes, _ = applied_ref.shape

    even = lax.rem(lax.axis_index("row"), 2) == 0
    copies = []
    for e in (0, 1):
        row = pl.ds(7 * e, 1)
        for o in range(orbitals):
            near, far = near_ref[pl.ds(o, 1), :], far_ref[pl.ds(o, 1), :]
            edge = jnp.where(even, near, far) if e else jnp.where(even, far, near)
            work_ref[e, o] = sides_ref[e, o]
            work_ref[e, o, row, :] = sides_ref[e, o, row, :] - 0.5 * edge
            target = out_ref.at[o, pl.ds(e * (planes - 8), 8), :]
            copies.append(pltpu.make_async_copy(work_ref.at[e, o], target, sem.at[e, o]))
            copies[-1].start()
    for copy in copies:
        copy.wait()


def fix_edges(applied, sides, near, far):
    orbitals, _, points = applied.shape
    return pl.pallas_call(
        fix_kernel,
        in_specs=[pl.BlockSpec(memory_space=pltpu.VMEM)] * 3 + [pl.BlockSpec(memory_space=pl.ANY)],
        out_specs=pl.BlockSpec(memory_space=pl.ANY),
        out_shape=jax.ShapeDtypeStruct(applied.shape, jnp.float32),
        input_output_aliases={3: 0},
        scratch_shapes=[
            pltpu.VMEM((2, orbitals, 8, points), jnp.float32),
            pltpu.SemaphoreType.DMA((2, orbitals)),
        ],
        compiler_params=pltpu.CompilerParams(vmem_limit_bytes=12 * 2**20),
        cost_estimate=pl.CostEstimate(flops=0, bytes_accessed=32 * orbitals * points, transcendentals=0),
    )(near, far, sides, applied)


def exchange(x, mask):
    every = ("row", "col")
    return lax.ppermute(x, every, [(i, i ^ mask) for i in range(lax.axis_size(every))])


def digit(position, radix):
    return (lax.axis_index(("row", "col")) // position) % radix


def reduce_digit(total, position):
    mine = digit(position, 4)
    parts = total.reshape(4, -1, total.shape[-1])
    pick = lambda k: lax.dynamic_index_in_dim(parts, mine ^ k, 0, keepdims=False)
    sent = [exchange(pick(k), k * position) for k in (1, 2, 3)]
    return pick(0) + sent[0] + sent[1] + sent[2]


def reduce_z_hi(total):
    parts = total.reshape(2, -1, total.shape[-1])
    mine = digit(16, 2)
    pick = lambda k: lax.dynamic_index_in_dim(parts, mine ^ k, 0, keepdims=False)
    z = lambda i: i // 8 % 4
    pairs = [(i, i + 8 * (3 - 2 * z(i))) for i in range(lax.axis_size(("row", "col")))]
    return pick(0) + lax.ppermute(pick(1), ("row", "col"), pairs)


def reduce_x(total, v):
    total = total.reshape(2, 4, -1, LANES)
    x = digit(2, 4)
    pick = lambda k: lax.dynamic_index_in_dim(total, x ^ k, 1, keepdims=False).reshape(-1, LANES)
    got = [exchange(jnp.concatenate([pick(k), v]), 2 * k) for k in (1, 2, 3)]
    height = got[0].shape[0] - v.shape[0]
    return sum([part[:height] for part in got], pick(0)), [v, *got]


def reduce_z_lo(total):
    total = total.reshape(2, -1, LANES)
    z = digit(8, 2)
    pick = lambda k: lax.dynamic_index_in_dim(total, z ^ k, 0, keepdims=False)
    return pick(0) + exchange(pick(1), 8)


def local(orbitals, potential):
    count, planes, points = orbitals.shape
    every = ("row", "col")
    devices, n_row, n_col = lax.axis_size(every), lax.axis_size("row"), lax.axis_size("col")
    rows = planes * points // LANES
    mine = count // n_col
    scale = 1.0 / (devices * planes * points)

    tiled = tile_view(orbitals).reshape(count * rows, LANES)
    v = tile_view(potential)
    to_core, to_chip = extract(tiled, count, rows)
    orbitals, to_core, to_chip, v = lax.optimization_barrier((orbitals, to_core, to_chip, v))
    v_z = jnp.concatenate([v, exchange(v, 8)])
    from_core = exchange(to_core, 1)
    from_chip = lax.ppermute(to_chip, every, [(i, (i + 1 ^ 1) - 1) for i in range(1, devices - 1)])
    received = lax.all_to_all(orbitals, "col", split_axis=0, concat_axis=0, tiled=True)
    received = tile_view(received.reshape(n_col, mine, planes, points)).reshape(n_col, mine * rows, LANES)

    g, by_core, by_chip = gram(tiled, v, count, rows)
    keep, send = finish(g, by_core, from_core, by_chip, from_chip, count, rows, scale)
    v_x = jnp.concatenate([v_z, exchange(v_z, 1)])
    g = reduce_digit(keep + exchange(send, 1), 32)
    g = reduce_z_hi(g)
    g, v_parts = reduce_x(g, v_x)

    near, far = edges_of(received, mine, rows)
    g, near, far = lax.optimization_barrier((g, near, far))
    near = lax.ppermute(near, "row", [(i, i ^ 1) for i in range(n_row)])
    far = lax.ppermute(far, "row", [(i, (i + 1 ^ 1) - 1) for i in range(1, n_row - 1)])
    relayed, applied, sides = to_block(received, v_parts, mine, rows)
    g = reduce_z_lo(g).reshape(planes, 2 * count)
    return g[:, :count], g[:, count:], relayed, fix_edges(applied, sides, near, far)


def solution(mesh):
    in_specs = (P(None, ("row", "col"), None), P(("row", "col"), None))
    out_specs = (
        P(("row", "col"), None),
        P(("row", "col"), None),
        P("col", "row", None),
        P("col", "row", None),
    )
    return jax.shard_map(local, mesh=mesh, in_specs=in_specs, out_specs=out_specs, check_vma=False)
```
